32 devices in a mesh: ctx: 8 (over y, x, core), ch: 4 (over z).
Axes of the slice: x: 2, y: 2, z: 4, core: 2. Of those that a mesh axis runs over, the one named last changes fastest.
Arguments:
- signal: bfloat16 [128, 131072], P('ch', 'ctx'), parts along dimension 0, may hold values from -6 to 6
- filter_taps: float32 [128, 131072], P('ch', 'ctx'), parts along dimension 0, may hold values from -0.015625 to 0.015625
- gate_values: bfloat16 [128, 131072], P('ch', 'ctx'), parts along dimension 0, may hold values from -6 to 6
- skip_gain: float32 [128], P('ch'), parts along dimension 0, may hold values from -4 to 4
Outputs:
- gated_output: bfloat16 [128, 131072], P('ch', 'ctx'), parts along dimension 0
The draws below stay inside these ranges and needn't reach their ends.
There are 4 independent parts, one for each index of `ch`. The reference program is written for one: setup_inputs(seed, part) draws one part's arguments, and reference() takes and returns one part's arrays. A program takes and returns all parts, laid end to end along the dimension named above; each array names one. Nothing has to cross between parts.
All inputs are finite; a program needn't handle non-finite values.
Results may differ from the reference program's by a relative error of at most 0.001.
Values sent between devices are 32-bit elements; how exact they have to be, the bound alone decides.
A program may use at most 128 MiB of HBM per device.

```python
import jax
import jax.numpy as jnp

CHANNELS = 32
SEQ = 131072


def block_levels(key, extent, split, least, top_value):
    gain = 1.0
    for position, shards_of in split:
        draws = jax.random.uniform(jax.random.fold_in(jax.random.fold_in(key, 6), position), (shards_of,), jnp.float32, least / len(split), top_value / len(split))
        gain = gain * jnp.repeat(jnp.exp(draws), extent[position] // shards_of).reshape((-1,) + (1,) * (len(extent) - 1 - position))
    return gain


def bell_draw(stream_key, extent, scale, most, shards=(), kind=jnp.bfloat16):
    gain = block_levels(stream_key, extent, shards, -0.22, 0.18) if shards else 1.0
    values = jax.random.normal(stream_key, extent, jnp.float32) * scale * gain
    return jnp.minimum(jnp.maximum(values, -most), most).astype(kind)


def setup_inputs(seed: int = 0, part: int = 0) -> dict:
    streams_of = jax.random.split(jax.random.key(seed), 5)
    own_keys = jax.random.split(jax.random.fold_in(streams_of[4], part), 5)
    signal = bell_draw(own_keys[0], (CHANNELS, SEQ), 1.0, 6.0, ((1, 8),))
    filter_taps = bell_draw(own_keys[1], (CHANNELS, SEQ), SEQ ** -0.5, 0.015625, ((1, 8),), jnp.float32)
    gate_values = bell_draw(own_keys[2], (CHANNELS, SEQ), 1.0, 6.0, ((1, 8),))
    skip_gain = bell_draw(own_keys[3], (CHANNELS,), 1.0, 4.0, (), jnp.float32)
    return {"signal": signal, "filter_taps": filter_taps, "gate_values": gate_values, "skip_gain": skip_gain}


def reference(signal, filter_taps, gate_values, skip_gain):
    length = signal.shape[1]
    inputs = signal.astype(jnp.float32)
    spectrum = jnp.fft.rfft(inputs, n=2 * length, axis=1) * jnp.fft.rfft(filter_taps, n=2 * length, axis=1)
    long_conv = jnp.fft.irfft(spectrum, n=2 * length, axis=1)[:, :length].astype(jnp.float32)
    gated = gate_values.astype(jnp.float32) * (long_conv + skip_gain[:, None] * inputs)
    return gated.astype(jnp.bfloat16)
```

```python
import functools
import math

import jax
import jax.numpy as jnp
import ml_dtypes
import numpy as np
from jax import lax
from jax.experimental import pallas as pl
from jax.experimental.pallas import tpu as pltpu
from jax.sharding import PartitionSpec as P

MESH = pl.DeviceIdType.MESH
BF16 = jnp.bfloat16
F32 = jnp.float32


def split_table(values):
    high = values.astype(ml_dtypes.bfloat16)
    low = (values - high.astype(np.float64)).astype(ml_dtypes.bfloat16)
    return high, low


def angles(rows, columns, period):
    return 2.0 * math.pi / period * (np.outer(rows, columns) % period)


def make_tables(first_len, second_len, chunk):
    chunks = first_len // chunk
    length = first_len * second_len
    first = np.arange(first_len, dtype=np.int64)
    second = np.arange(second_len, dtype=np.int64)
    quarter = 4 * first + 1
    theta = angles(quarter, first, 4 * first_len)
    forward = np.stack([np.cos(theta), -np.sin(theta)]).reshape(2, chunks, chunk, first_len)
    forward = forward.transpose(1, 0, 2, 3).reshape(chunks, 2 * chunk, first_len)
    backward = np.ascontiguousarray(forward.transpose(0, 2, 1))
    theta = angles(quarter, second, 4 * length)
    twist = np.stack([np.cos(theta), -np.sin(theta)]).reshape(2, chunks, chunk, second_len)
    twist = np.ascontiguousarray(twist.transpose(1, 0, 2, 3)).astype(np.float32)
    theta = angles(second, second, second_len)
    cos, sin = np.cos(theta), np.sin(theta)
    inner = np.block([[cos, -sin], [sin, cos]])
    return (*split_table(forward), *split_table(backward), *split_table(inner), twist)


def split(values):
    high = values.astype(BF16)
    low = (values - high.astype(F32)).astype(BF16)
    return high, low


def dot(left, right):
    return jnp.dot(left, right, preferred_element_type=F32)


def kernel(devices, chunk, sf_ref, *refs):
    tables, (out_ref,), rest = refs[:7], refs[7:8], refs[8:]
    held, rest = rest[:7], rest[7:]
    got, wide, send_sem, recv_sem, own_sem, table_sem, back_send, back_recv, back_own = rest
    fwd_hi, fwd_lo, bwd_hi, bwd_lo, in_hi, in_lo, twist = held
    me = lax.axis_index("ctx")
    _, channels, _, rows, width = sf_ref.shape
    chunks = fwd_hi.shape[0]
    scale = 1.0 / (devices * rows * width)

    def peer(step):
        return lax.rem(me + step, devices)

    barrier = pltpu.get_barrier_semaphore()
    for step in range(1, devices):
        pl.semaphore_signal(barrier, inc=1, device_id={"ctx": peer(step)}, device_id_type=MESH)
    pl.semaphore_wait(barrier, devices - 1)

    def own_rows(device):
        return pl.ds(pl.multiple_of(device * rows, rows), rows)

    def outward(channel, step):
        return pltpu.make_async_remote_copy(
            src_ref=sf_ref.at[peer(step), channel],
            dst_ref=got.at[channel, :, own_rows(me), :],
            send_sem=send_sem.at[channel, step],
            recv_sem=recv_sem.at[channel, step],
            device_id={"ctx": peer(step)},
            device_id_type=MESH,
        )

    def outward_own(channel):
        return pltpu.make_async_copy(
            sf_ref.at[me, channel], got.at[channel, :, own_rows(me), :], own_sem.at[channel]
        )

    def inward(channel, step):
        return pltpu.make_async_remote_copy(
            src_ref=got.at[channel, 0, own_rows(peer(step)), :],
            dst_ref=out_ref.at[me, channel],
            send_sem=back_send.at[channel, step],
            recv_sem=back_recv.at[channel, step],
            device_id={"ctx": peer(step)},
            device_id_type=MESH,
        )

    def inward_own(channel):
        return pltpu.make_async_copy(
            got.at[channel, 0, own_rows(me), :], out_ref.at[me, channel], back_own.at[channel]
        )

    for channel in range(channels):
        for step in range(1, devices):
            outward(channel, step).start()
        outward_own(channel).start()
    loads = [
        pltpu.make_async_copy(source, target, table_sem.at[i])
        for i, (source, target) in enumerate(zip(tables, held))
    ]
    for load in loads:
        load.start()
    for load in loads:
        load.wait()

    def one_channel(channel, carry):
        outward_own(channel).wait()
        for step in range(1, devices):
            outward(channel, step).wait_recv()
        high, low = split(got[channel, 1])
        wide[:, :width] = got[channel, 0].astype(BF16)
        wide[:, width : 2 * width] = high
        wide[:, 2 * width :] = low

        def one_chunk(part, carry):
            from_high = dot(fwd_hi[part], wide[...])
            from_low = dot(fwd_lo[part], wide[:, : 2 * width])
            both = from_high[:, : 2 * width] + from_low
            series = (both[:, :width], both[:, width:] + from_high[:, 2 * width :])
            cos, sin = twist[part, 0], twist[part, 1]
            turned = [
                jnp.concatenate(
                    [
                        value[:chunk] * cos - value[chunk:] * sin,
                        value[:chunk] * sin + value[chunk:] * cos,
                    ],
                    axis=1,
                )
                for value in series
            ]
            high, low = split(jnp.concatenate(turned, axis=0))
            bins = dot(high, in_hi[...]) + dot(high, in_lo[...]) + dot(low, in_hi[...])
            s_re, s_im = bins[:chunk, :width], bins[:chunk, width:]
            f_re, f_im = bins[chunk:, :width] * scale, bins[chunk:, width:] * scale
            prod = jnp.concatenate(
                [s_re * f_re - s_im * f_im, -(s_re * f_im + s_im * f_re)], axis=1
            )
            high, low = split(prod)
            back = dot(high, in_hi[...]) + dot(high, in_lo[...]) + dot(low, in_hi[...])
            b_re, b_im = back[:, :width], back[:, width:]
            high, low = split(
                jnp.concatenate([b_re * cos - b_im * sin, -(b_re * sin + b_im * cos)], axis=0)
            )
            term = dot(bwd_hi[part], high) + dot(bwd_lo[part], high) + dot(bwd_hi[part], low)

            @pl.when(part == 0)
            def _():
                got[channel, 0] = term

            @pl.when(part > 0)
            def _():
                got[channel, 0] += term

            return carry

        lax.fori_loop(0, chunks, one_chunk, 0)
        for step in range(1, devices):
            inward(channel, step).start()
        inward_own(channel).start()
        return carry

    lax.fori_loop(0, channels, one_channel, 0)
    for channel in range(channels):
        inward_own(channel).wait()
        for step in range(1, devices):
            outward(channel, step).wait_send()
            inward(channel, step).wait_send()
            inward(channel, step).wait_recv()


def shards(signal, filter_taps, gate_values, skip_gain):
    devices = lax.axis_size("ctx")
    channels, block = signal.shape
    length = devices * block
    own = channels // devices
    second_len = 1
    while 4 * second_len * second_len <= length:
        second_len *= 2
    first_len = length // second_len
    rows = first_len // devices
    chunk = min(first_len, max(128, 131072 // first_len))
    tables = make_tables(first_len, second_len, chunk)
    inputs = signal.astype(F32)
    shape = (devices, own, rows, second_len)
    packed = jnp.stack([inputs.reshape(shape), filter_taps.reshape(shape)], axis=2)
    anywhere = pl.BlockSpec(memory_space=pl.ANY)
    pairs = pltpu.SemaphoreType.DMA((own, devices))
    singles = pltpu.SemaphoreType.DMA((own,))
    long_conv = pl.pallas_call(
        functools.partial(kernel, devices, chunk),
        out_shape=jax.ShapeDtypeStruct(shape, F32),
        in_specs=[anywhere] * 8,
        out_specs=anywhere,
        scratch_shapes=[pltpu.VMEM(table.shape, table.dtype) for table in tables]
        + [
            pltpu.VMEM((own, 2, first_len, second_len), F32),
            pltpu.VMEM((first_len, 3 * second_len), BF16),
            pairs,
            pairs,
            singles,
            pltpu.SemaphoreType.DMA((7,)),
            pairs,
            pairs,
            singles,
        ],
        compiler_params=pltpu.CompilerParams(
            collective_id=0, has_side_effects=True, vmem_limit_bytes=60 * 1024 * 1024
        ),
    )(packed, *[jnp.asarray(table) for table in tables])
    long_conv = long_conv.reshape(channels, block)
    gated = gate_values.astype(F32) * (long_conv + skip_gain[:, None] * inputs)
    return gated.astype(BF16)


def solution(mesh):
    in_specs = (P("ch", "ctx"), P("ch", "ctx"), P("ch", "ctx"), P("ch"))
    out_specs = P("ch", "ctx")
    return jax.shard_map(shards, mesh=mesh, in_specs=in_specs, out_specs=out_specs, check_vma=False)
```

```python
import functools
import math

import jax
import jax.numpy as jnp
import ml_dtypes
import numpy as np
from jax import lax
from jax.experimental import pallas as pl
from jax.experimental.pallas import tpu as pltpu
from jax.sharding import PartitionSpec as P

MESH = pl.DeviceIdType.MESH
BF16 = jnp.bfloat16
F32 = jnp.float32


def split_table(values):
    high = values.astype(ml_dtypes.bfloat16)
    low = (values - high.astype(np.float64)).astype(ml_dtypes.bfloat16)
    return high, low


def angles(rows, columns, period):
    return 2.0 * math.pi / period * (np.outer(rows, columns) % period)


def make_tables(first_len, second_len, chunk):
    chunks = first_len // chunk
    length = first_len * second_len
    first = np.arange(first_len, dtype=np.int64)
    second = np.arange(second_len, dtype=np.int64)
    quarter = 4 * first + 1
    theta = angles(quarter, first, 4 * first_len)
    forward = np.stack([np.cos(theta), -np.sin(theta)]).reshape(2, chunks, chunk, first_len)
    forward = forward.transpose(1, 0, 2, 3).reshape(chunks, 2 * chunk, first_len)
    backward = np.ascontiguousarray(forward.transpose(0, 2, 1))
    theta = angles(quarter, second, 4 * length)
    twist = np.stack([np.cos(theta), -np.sin(theta)]).reshape(2, chunks, chunk, second_len)
    twist = np.ascontiguousarray(twist.transpose(1, 0, 2, 3)).astype(np.float32)
    theta = angles(second, second, second_len)
    cos, sin = np.cos(theta), np.sin(theta)
    inner = np.block([[cos, -sin], [sin, cos]])
    return (*split_table(forward), *split_table(backward), *split_table(inner), twist)


def split(values):
    high = values.astype(BF16)
    low = (values - high.astype(F32)).astype(BF16)
    return high, low


def dot(left, right):
    return jnp.dot(left, right, preferred_element_type=F32)


def kernel(devices, chunk, fused, *refs):
    tables, rest = refs[:7], refs[7:]
    held = rest[-16:-9]
    got, wide, send_sem, recv_sem, own_sem, table_sem, back_send, back_recv, back_own = rest[-9:]
    if fused:
        signal_ref, taps_ref, gate_ref, skip_ref, out_ref = rest[:5]
        signal, taps, gate, result, tile_s, tile_f, sf_ref, back_ref, load_sem = rest[5:-16]
    else:
        sf_ref, back_ref = rest[:2]
    fwd_hi, fwd_lo, bwd_hi, bwd_lo, in_hi, in_lo, twist = held
    me = lax.axis_index("ctx")
    _, channels, _, rows, width = sf_ref.shape
    chunks = fwd_hi.shape[0]
    scale = 1.0 / (devices * rows * width)
    folds = width // 128
    lanes = devices * channels

    def peer(step):
        return lax.rem(me + step, devices)

    if fused:
        arrivals = [
            pltpu.make_async_copy(source, target, load_sem.at[i])
            for i, (source, target) in enumerate(
                ((taps_ref, taps), (signal_ref, signal), (gate_ref, gate))
            )
        ]
        for arrival in arrivals:
            arrival.start()

    barrier = pltpu.get_barrier_semaphore()
    for step in range(1, devices):
        pl.semaphore_signal(barrier, inc=1, device_id={"ctx": peer(step)}, device_id_type=MESH)

    def tile(column):
        return pl.ds(pl.multiple_of(column * 128, 128), 128)

    def tile_rows(column):
        return pl.ds(pl.multiple_of(column * lanes, lanes), lanes)

    if fused:
        columns = rows * folds
        arrivals[0].wait()

        def lay_taps(column, carry):
            tile_f[tile_rows(column), :] = taps[:, tile(column)]
            return carry

        lax.fori_loop(0, columns, lay_taps, 0, unroll=8)
        arrivals[1].wait()

        def lay_signal(column, carry):
            tile_s[tile_rows(column), :] = signal[:, tile(column)].astype(F32)
            return carry

        lax.fori_loop(0, columns, lay_signal, 0, unroll=8)

    pl.semaphore_wait(barrier, devices - 1)

    def strip(device, channel, fold):
        start = device * channels + channel + fold * lanes
        return pl.ds(start, rows, stride=lanes * folds)

    def own_rows(device):
        return pl.ds(pl.multiple_of(device * rows, rows), rows)

    def outward(channel, step):
        return pltpu.make_async_remote_copy(
            src_ref=sf_ref.at[peer(step), channel],
            dst_ref=got.at[channel, :, own_rows(me), :],
            send_sem=send_sem.at[channel, step],
            recv_sem=recv_sem.at[channel, step],
            device_id={"ctx": peer(step)},
            device_id_type=MESH,
        )

    def outward_own(channel):
        return pltpu.make_async_copy(
            sf_ref.at[me, channel], got.at[channel, :, own_rows(me), :], own_sem.at[channel]
        )

    def inward(channel, step):
        return pltpu.make_async_remote_copy(
            src_ref=got.at[channel, 0, own_rows(peer(step)), :],
            dst_ref=back_ref.at[me, channel],
            send_sem=back_send.at[channel, step],
            recv_sem=back_recv.at[channel, step],
            device_id={"ctx": peer(step)},
            device_id_type=MESH,
        )

    def inward_own(channel):
        return pltpu.make_async_copy(
            got.at[channel, 0, own_rows(me), :], back_ref.at[me, channel], back_own.at[channel]
        )

    for channel in range(channels):
        if fused:
            for device in range(devices):
                for fold in range(folds):
                    part = pl.ds(fold * 128, 128)
                    where = strip(device, channel, fold)
                    sf_ref[device, channel, 0, :, part] = tile_s[where, :]
                    sf_ref[device, channel, 1, :, part] = tile_f[where, :]
        for step in range(1, devices):
            outward(channel, step).start()
        outward_own(channel).start()
    loads = [
        pltpu.make_async_copy(source, target, table_sem.at[i])
        for i, (source, target) in enumerate(zip(tables, held))
    ]
    for load in loads:
        load.start()
    for load in loads:
        load.wait()

    def one_channel(channel, carry):
        outward_own(channel).wait()
        for step in range(1, devices):
            outward(channel, step).wait_recv()
        high, low = split(got[channel, 1])
        wide[:, :width] = got[channel, 0].astype(BF16)
        wide[:, width : 2 * width] = high
        wide[:, 2 * width :] = low

        def one_chunk(part, carry):
            from_high = dot(fwd_hi[part], wide[...])
            from_low = dot(fwd_lo[part], wide[:, : 2 * width])
            both = from_high[:, : 2 * width] + from_low
            series = (both[:, :width], both[:, width:] + from_high[:, 2 * width :])
            cos, sin = twist[part, 0], twist[part, 1]
            turned = [
                jnp.concatenate(
                    [
                        value[:chunk] * cos - value[chunk:] * sin,
                        value[:chunk] * sin + value[chunk:] * cos,
                    ],
                    axis=1,
                )
                for value in series
            ]
            high, low = split(jnp.concatenate(turned, axis=0))
            bins = dot(high, in_hi[...]) + dot(high, in_lo[...]) + dot(low, in_hi[...])
            s_re, s_im = bins[:chunk, :width], bins[:chunk, width:]
            f_re, f_im = bins[chunk:, :width] * scale, bins[chunk:, width:] * scale
            prod = jnp.concatenate(
                [s_re * f_re - s_im * f_im, -(s_re * f_im + s_im * f_re)], axis=1
            )
            high, low = split(prod)
            back = dot(high, in_hi[...]) + dot(high, in_lo[...]) + dot(low, in_hi[...])
            b_re, b_im = back[:, :width], back[:, width:]
            high, low = split(
                jnp.concatenate([b_re * cos - b_im * sin, -(b_re * sin + b_im * cos)], axis=0)
            )
            term = dot(bwd_hi[part], high) + dot(bwd_lo[part], high) + dot(bwd_hi[part], low)

            @pl.when(part == 0)
            def _():
                got[channel, 0] = term

            @pl.when(part > 0)
            def _():
                got[channel, 0] += term

            return carry

        lax.fori_loop(0, chunks, one_chunk, 0)
        for step in range(1, devices):
            inward(channel, step).start()
        inward_own(channel).start()
        return carry

    lax.fori_loop(0, channels, one_channel, 0)
    for channel in range(channels):
        inward_own(channel).wait()
        for step in range(1, devices):
            inward(channel, step).wait_recv()
        if fused:
            for device in range(devices):
                for fold in range(folds):
                    part = pl.ds(fold * 128, 128)
                    tile_s[strip(device, channel, fold), :] = back_ref[device, channel, :, part]
    if fused:
        arrivals[2].wait()

        def finish(column, carry):
            there = tile(column)
            total = tile_s[tile_rows(column), :] + skip_ref[...] * signal[:, there].astype(F32)
            result[:, there] = (gate[:, there].astype(F32) * total).astype(BF16)
            return carry

        lax.fori_loop(0, columns, finish, 0, unroll=8)
        leave = pltpu.make_async_copy(result, out_ref, load_sem.at[3])
        leave.start()
        leave.wait()
    for channel in range(channels):
        for step in range(1, devices):
            outward(channel, step).wait_send()
            inward(channel, step).wait_send()


def shards(signal, filter_taps, gate_values, skip_gain):
    devices = lax.axis_size("ctx")
    channels, block = signal.shape
    length = devices * block
    own = channels // devices
    second_len = 1
    while 4 * second_len * second_len <= length:
        second_len *= 2
    first_len = length // second_len
    rows = first_len // devices
    chunk = min(first_len, max(128, 131072 // first_len))
    tables = make_tables(first_len, second_len, chunk)
    fused = channels * block <= 1 << 19
    shape = (devices, own, rows, second_len)
    packed_shape = (devices, own, 2, rows, second_len)
    anywhere = pl.BlockSpec(memory_space=pl.ANY)
    pairs = pltpu.SemaphoreType.DMA((own, devices))
    singles = pltpu.SemaphoreType.DMA((own,))
    scratch = [pltpu.VMEM(table.shape, table.dtype) for table in tables] + [
        pltpu.VMEM((own, 2, first_len, second_len), F32),
        pltpu.VMEM((first_len, 3 * second_len), BF16),
        pairs,
        pairs,
        singles,
        pltpu.SemaphoreType.DMA((7,)),
        pairs,
        pairs,
        singles,
    ]
    if fused:
        scratch = [
            pltpu.VMEM((channels, block), BF16),
            pltpu.VMEM((channels, block), F32),
            pltpu.VMEM((channels, block), BF16),
            pltpu.VMEM((channels, block), BF16),
            pltpu.VMEM((channels * block // 128, 128), F32),
            pltpu.VMEM((channels * block // 128, 128), F32),
            pltpu.VMEM(packed_shape, F32),
            pltpu.VMEM(shape, F32),
            pltpu.SemaphoreType.DMA((4,)),
        ] + scratch
        gains = jnp.broadcast_to(skip_gain[:, None], (channels, 128))
        operands = [signal, filter_taps, gate_values, gains]
        specs = [anywhere] * 3 + [pl.BlockSpec(memory_space=pltpu.VMEM)]
        out_shape = jax.ShapeDtypeStruct((channels, block), BF16)
    else:
        inputs = signal.astype(F32)
        operands = [jnp.stack([inputs.reshape(shape), filter_taps.reshape(shape)], axis=2)]
        specs = [anywhere]
        out_shape = jax.ShapeDtypeStruct(shape, F32)
    result = pl.pallas_call(
        functools.partial(kernel, devices, chunk, fused),
        out_shape=out_shape,
        in_specs=[anywhere] * 7 + specs,
        out_specs=anywhere,
        scratch_shapes=scratch,
        compiler_params=pltpu.CompilerParams(
            collective_id=0, has_side_effects=True, vmem_limit_bytes=60 * 1024 * 1024
        ),
    )(*[jnp.asarray(table) for table in tables], *operands)
    if fused:
        return result
    long_conv = result.reshape(channels, block)
    gated = gate_values.astype(F32) * (long_conv + skip_gain[:, None] * inputs)
    return gated.astype(BF16)


def solution(mesh):
    in_specs = (P("ch", "ctx"), P("ch", "ctx"), P("ch", "ctx"), P("ch"))
    out_specs = P("ch", "ctx")
    return jax.shard_map(shards, mesh=mesh, in_specs=in_specs, out_specs=out_specs, check_vma=False)
```

```python
import functools
import math

import jax
import jax.numpy as jnp
import ml_dtypes
import numpy as np
from jax import lax
from jax.experimental import pallas as pl
from jax.experimental.pallas import tpu as pltpu
from jax.sharding import PartitionSpec as P

MESH = pl.DeviceIdType.MESH
BF16 = jnp.bfloat16
F32 = jnp.float32


def split_table(values):
    high = values.astype(ml_dtypes.bfloat16)
    low = (values - high.astype(np.float64)).astype(ml_dtypes.bfloat16)
    return high, low


def angles(rows, columns, period):
    return 2.0 * math.pi / period * (np.outer(rows, columns) % period)


def make_tables(first_len, second_len, chunk):
    chunks = first_len // chunk
    length = first_len * second_len
    first = np.arange(first_len, dtype=np.int64)
    second = np.arange(second_len, dtype=np.int64)
    quarter = 4 * first + 1
    theta = angles(quarter, first, 4 * first_len)
    forward = np.stack([np.cos(theta), -np.sin(theta)]).reshape(2, chunks, chunk, first_len)
    forward = forward.transpose(1, 0, 2, 3).reshape(chunks, 2 * chunk, first_len)
    backward = np.ascontiguousarray(forward.transpose(0, 2, 1))
    theta = angles(quarter, second, 4 * length)
    twist = np.stack([np.cos(theta), -np.sin(theta)]).reshape(2, chunks, chunk, second_len)
    twist = np.ascontiguousarray(twist.transpose(1, 0, 2, 3)).astype(np.float32)
    theta = angles(second, second, second_len)
    cos, sin = np.cos(theta), np.sin(theta)
    inner = np.block([[cos, -sin], [sin, cos]])
    return (*split_table(forward), *split_table(backward), *split_table(inner), twist)


def split(values):
    high = values.astype(BF16)
    low = (values - high.astype(F32)).astype(BF16)
    return high, low


def dot(left, right):
    return jnp.dot(left, right, preferred_element_type=F32)


def kernel(devices, chunk, fused, *refs):
    tables, rest = refs[:7], refs[7:]
    held = rest[-16:-9]
    got, wide, send_sem, recv_sem, own_sem, table_sem, back_send, back_recv, back_own = rest[-9:]
    if fused:
        signal_ref, taps_ref, out_ref = rest[:3]
        signal, taps, result, tile_s, tile_f, sf_ref, back_ref, load_sem = rest[3:-16]
    else:
        sf_ref, back_ref = rest[:2]
    fwd_hi, fwd_lo, bwd_hi, bwd_lo, in_hi, in_lo, twist = held
    me = lax.axis_index("ctx")
    _, channels, _, rows, width = sf_ref.shape
    chunks = fwd_hi.shape[0]
    scale = 1.0 / (devices * rows * width)
    folds = width // 128
    lanes = devices * channels

    def peer(step):
        return lax.rem(me + step, devices)

    if fused:
        arrivals = [
            pltpu.make_async_copy(source, target, load_sem.at[i])
            for i, (source, target) in enumerate(
                ((taps_ref, taps), (signal_ref, signal))
            )
        ]
        for arrival in arrivals:
            arrival.start()

    barrier = pltpu.get_barrier_semaphore()
    for step in range(1, devices):
        pl.semaphore_signal(barrier, inc=1, device_id={"ctx": peer(step)}, device_id_type=MESH)

    def tile(column):
        return pl.ds(pl.multiple_of(column * 128, 128), 128)

    def tile_rows(column):
        return pl.ds(pl.multiple_of(column * lanes, lanes), lanes)

    if fused:
        columns = rows * folds
        arrivals[0].wait()

        def lay_taps(column, carry):
            tile_f[tile_rows(column), :] = taps[:, tile(column)]
            return carry

        lax.fori_loop(0, columns, lay_taps, 0, unroll=8)
        arrivals[1].wait()

        def lay_signal(column, carry):
            tile_s[tile_rows(column), :] = signal[:, tile(column)].astype(F32)
            return carry

        lax.fori_loop(0, columns, lay_signal, 0, unroll=8)

    pl.semaphore_wait(barrier, devices - 1)

    def strip(device, channel, fold):
        start = device * channels + channel + fold * lanes
        return pl.ds(start, rows, stride=lanes * folds)

    def own_rows(device):
        return pl.ds(pl.multiple_of(device * rows, rows), rows)

    def outward(channel, which, step):
        return pltpu.make_async_remote_copy(
            src_ref=sf_ref.at[peer(step), channel, which],
            dst_ref=got.at[channel, which, own_rows(me), :],
            send_sem=send_sem.at[channel, which, step],
            recv_sem=recv_sem.at[channel, which, step],
            device_id={"ctx": peer(step)},
            device_id_type=MESH,
        )

    def outward_own(channel):
        return pltpu.make_async_copy(
            sf_ref.at[me, channel], got.at[channel, :, own_rows(me), :], own_sem.at[channel]
        )

    def inward(channel, step):
        return pltpu.make_async_remote_copy(
            src_ref=got.at[channel, 0, own_rows(peer(step)), :],
            dst_ref=back_ref.at[me, channel],
            send_sem=back_send.at[channel, step],
            recv_sem=back_recv.at[channel, step],
            device_id={"ctx": peer(step)},
            device_id_type=MESH,
        )

    def inward_own(channel):
        return pltpu.make_async_copy(
            got.at[channel, 0, own_rows(me), :], back_ref.at[me, channel], back_own.at[channel]
        )

    others = [(which, step) for which in range(2) for step in range(1, devices)]

    for channel in range(channels):
        if fused:
            for device in range(devices):
                for fold in range(folds):
                    part = pl.ds(fold * 128, 128)
                    where = strip(device, channel, fold)
                    sf_ref[device, channel, 0, :, part] = tile_s[where, :]
                    sf_ref[device, channel, 1, :, part] = tile_f[where, :]
        if channel == 0:
            for which, step in others:
                outward(channel, which, step).start()
        outward_own(channel).start()
    loads = [
        pltpu.make_async_copy(source, target, table_sem.at[i])
        for i, (source, target) in enumerate(zip(tables, held))
    ]
    for load in loads:
        load.start()
    for load in loads:
        load.wait()

    def arrive(channel):
        outward_own(channel).wait()
        for which, step in others:
            outward(channel, which, step).wait_recv()

    def give_back(channel):
        for step in range(1, devices):
            inward(channel, step).start()
        inward_own(channel).start()

    def convolve(channel):
        high, low = split(got[channel, 1])
        wide[:, :width] = got[channel, 0].astype(BF16)
        wide[:, width : 2 * width] = high
        wide[:, 2 * width :] = low

        def one_chunk(part, carry):
            from_high = dot(fwd_hi[part], wide[...])
            from_low = dot(fwd_lo[part], wide[:, : 2 * width])
            both = from_high[:, : 2 * width] + from_low
            series = (both[:, :width], both[:, width:] + from_high[:, 2 * width :])
            cos, sin = twist[part, 0], twist[part, 1]
            turned = [
                jnp.concatenate(
                    [
                        value[:chunk] * cos - value[chunk:] * sin,
                        value[:chunk] * sin + value[chunk:] * cos,
                    ],
                    axis=1,
                )
                for value in series
            ]
            high, low = split(jnp.concatenate(turned, axis=0))
            bins = dot(high, in_hi[...]) + dot(high, in_lo[...]) + dot(low, in_hi[...])
            s_re, s_im = bins[:chunk, :width], bins[:chunk, width:]
            f_re, f_im = bins[chunk:, :width] * scale, bins[chunk:, width:] * scale
            prod = jnp.concatenate(
                [s_re * f_re - s_im * f_im, -(s_re * f_im + s_im * f_re)], axis=1
            )
            high, low = split(prod)
            back = dot(high, in_hi[...]) + dot(high, in_lo[...]) + dot(low, in_hi[...])
            b_re, b_im = back[:, :width], back[:, width:]
            high, low = split(
                jnp.concatenate([b_re * cos - b_im * sin, -(b_re * sin + b_im * cos)], axis=0)
            )
            term = dot(bwd_hi[part], high) + dot(bwd_lo[part], high) + dot(bwd_hi[part], low)

            @pl.when(part == 0)
            def _():
                got[channel, 0] = term

            @pl.when(part > 0)
            def _():
                got[channel, 0] += term

            return carry

        lax.fori_loop(0, chunks, one_chunk, 0)

    def one_channel(channel, carry):
        for which, step in others:
            outward(channel, which, step).wait_send()
            outward(channel + 1, which, step).start()
        arrive(channel)
        convolve(channel)
        return carry

    last = channels - 1
    lax.fori_loop(0, last, one_channel, 0)
    for which, step in others:
        outward(last, which, step).wait_send()
    arrive(last)
    for channel in range(last):
        give_back(channel)
    convolve(last)
    give_back(last)
    for channel in range(channels):
        inward_own(channel).wait()
        for step in range(1, devices):
            inward(channel, step).wait_recv()
        if fused:
            for device in range(devices):
                for fold in range(folds):
                    part = pl.ds(fold * 128, 128)
                    tile_s[strip(device, channel, fold), :] = back_ref[device, channel, :, part]
    if fused:
        pieces = 4
        span = columns // pieces
        leaves = []

        def finish(column, carry):
            result[:, tile(column)] = tile_s[tile_rows(column), :]
            return carry

        for piece in range(pieces):
            lax.fori_loop(piece * span, (piece + 1) * span, finish, 0, unroll=8)
            there = pl.ds(piece * span * 128, span * 128)
            leaves.append(
                pltpu.make_async_copy(
                    result.at[:, there], out_ref.at[:, there], load_sem.at[2 + piece]
                )
            )
            leaves[-1].start()
        for leave in leaves:
            leave.wait()
    for channel in range(channels):
        for step in range(1, devices):
            inward(channel, step).wait_send()


def shards(signal, filter_taps, gate_values, skip_gain):
    devices = lax.axis_size("ctx")
    channels, block = signal.shape
    length = devices * block
    own = channels // devices
    second_len = 1
    while 4 * second_len * second_len <= length:
        second_len *= 2
    first_len = length // second_len
    rows = first_len // devices
    chunk = min(first_len, max(128, 131072 // first_len))
    tables = make_tables(first_len, second_len, chunk)
    inputs = signal.astype(F32)
    fused = channels * block <= 1 << 19
    shape = (devices, own, rows, second_len)
    packed_shape = (devices, own, 2, rows, second_len)
    anywhere = pl.BlockSpec(memory_space=pl.ANY)
    out_pairs = pltpu.SemaphoreType.DMA((own, 2, devices))
    pairs = pltpu.SemaphoreType.DMA((own, devices))
    singles = pltpu.SemaphoreType.DMA((own,))
    scratch = [pltpu.VMEM(table.shape, table.dtype) for table in tables] + [
        pltpu.VMEM((own, 2, first_len, second_len), F32),
        pltpu.VMEM((first_len, 3 * second_len), BF16),
        out_pairs,
        out_pairs,
        singles,
        pltpu.SemaphoreType.DMA((7,)),
        pairs,
        pairs,
        singles,
    ]
    if fused:
        scratch = [
            pltpu.VMEM((channels, block), BF16),
            pltpu.VMEM((channels, block), F32),
            pltpu.VMEM((channels, block), F32),
            pltpu.VMEM((channels * block // 128, 128), F32),
            pltpu.VMEM((channels * block // 128, 128), F32),
            pltpu.VMEM(packed_shape, F32),
            pltpu.VMEM(shape, F32),
            pltpu.SemaphoreType.DMA((6,)),
        ] + scratch
        operands = [signal, filter_taps]
        out_shape = jax.ShapeDtypeStruct((channels, block), F32)
    else:
        operands = [jnp.stack([inputs.reshape(shape), filter_taps.reshape(shape)], axis=2)]
        out_shape = jax.ShapeDtypeStruct(shape, F32)
    result = pl.pallas_call(
        functools.partial(kernel, devices, chunk, fused),
        out_shape=out_shape,
        in_specs=[anywhere] * (7 + len(operands)),
        out_specs=anywhere,
        scratch_shapes=scratch,
        compiler_params=pltpu.CompilerParams(
            collective_id=0, has_side_effects=True, vmem_limit_bytes=60 * 1024 * 1024
        ),
    )(*[jnp.asarray(table) for table in tables], *operands)
    long_conv = result.reshape(channels, block)
    gated = gate_values.astype(F32) * (long_conv + skip_gain[:, None] * inputs)
    return gated.astype(BF16)


def solution(mesh):
    in_specs = (P("ch", "ctx"), P("ch", "ctx"), P("ch", "ctx"), P("ch"))
    out_specs = P("ch", "ctx")
    return jax.shard_map(shards, mesh=mesh, in_specs=in_specs, out_specs=out_specs, check_vma=False)
```

```python
import functools
import math

import jax
import jax.numpy as jnp
import ml_dtypes
import numpy as np
from jax import lax
from jax.experimental import pallas as pl
from jax.experimental.pallas import tpu as pltpu
from jax.sharding import PartitionSpec as P

MESH = pl.DeviceIdType.MESH
BF16 = jnp.bfloat16
F32 = jnp.float32


def split_table(values):
    high = values.astype(ml_dtypes.bfloat16)
    low = (values - high.astype(np.float64)).astype(ml_dtypes.bfloat16)
    return high, low


def angles(rows, columns, period):
    return 2.0 * math.pi / period * (np.outer(rows, columns) % period)


def make_tables(first_len, second_len, chunk):
    chunks = first_len // chunk
    length = first_len * second_len
    first = np.arange(first_len, dtype=np.int64)
    second = np.arange(second_len, dtype=np.int64)
    quarter = 4 * first + 1
    theta = angles(quarter, first, 4 * first_len)
    forward = np.stack([np.cos(theta), -np.sin(theta)]).reshape(2, chunks, chunk, first_len)
    forward = forward.transpose(1, 0, 2, 3).reshape(chunks, 2 * chunk, first_len)
    backward = np.ascontiguousarray(forward.transpose(0, 2, 1))
    theta = angles(quarter, second, 4 * length)
    twist = np.stack([np.cos(theta), -np.sin(theta)]).reshape(2, chunks, chunk, second_len)
    twist = np.ascontiguousarray(twist.transpose(1, 0, 2, 3)).astype(np.float32)
    theta = angles(second, second, second_len)
    cos, sin = np.cos(theta), np.sin(theta)
    inner = np.block([[cos, -sin], [sin, cos]])
    return (*split_table(forward), *split_table(backward), *split_table(inner), twist)


def split(values):
    high = values.astype(BF16)
    low = (values - high.astype(F32)).astype(BF16)
    return high, low


def dot(left, right):
    return jnp.dot(left, right, preferred_element_type=F32)


def kernel(devices, chunk, fused, *refs):
    tables, rest = refs[:7], refs[7:]
    held = rest[-16:-9]
    got, wide, send_sem, recv_sem, own_sem, table_sem, back_send, back_recv, back_own = rest[-9:]
    if fused:
        signal_ref, taps_ref, out_ref = rest[:3]
        signal, taps, result, tile_s, tile_f, sf_ref, back_ref, load_sem = rest[3:-16]
    else:
        sf_ref, back_ref = rest[:2]
    fwd_hi, fwd_lo, bwd_hi, bwd_lo, in_hi, in_lo, twist = held
    me = lax.axis_index("ctx")
    _, channels, _, rows, width = sf_ref.shape
    chunks = fwd_hi.shape[0]
    scale = 1.0 / (devices * rows * width)
    folds = width // 128
    lanes = devices * channels

    def peer(step):
        return lax.rem(me + step, devices)

    if fused:
        arrivals = [
            pltpu.make_async_copy(source, target, load_sem.at[i])
            for i, (source, target) in enumerate(
                ((taps_ref, taps), (signal_ref, signal))
            )
        ]
        for arrival in arrivals:
            arrival.start()

    barrier = pltpu.get_barrier_semaphore()
    for step in range(1, devices):
        pl.semaphore_signal(barrier, inc=1, device_id={"ctx": peer(step)}, device_id_type=MESH)

    def tile(column):
        return pl.ds(pl.multiple_of(column * 128, 128), 128)

    def tile_rows(column):
        return pl.ds(pl.multiple_of(column * lanes, lanes), lanes)

    if fused:
        columns = rows * folds
        arrivals[0].wait()

        def lay_taps(column, carry):
            tile_f[tile_rows(column), :] = taps[:, tile(column)]
            return carry

        lax.fori_loop(0, columns, lay_taps, 0, unroll=8)

    pl.semaphore_wait(barrier, devices - 1)

    def strip(device, channel, fold):
        start = device * channels + channel + fold * lanes
        return pl.ds(start, rows, stride=lanes * folds)

    def own_rows(device):
        return pl.ds(pl.multiple_of(device * rows, rows), rows)

    def outward(channel, which, step):
        return pltpu.make_async_remote_copy(
            src_ref=sf_ref.at[peer(step), channel, which],
            dst_ref=got.at[channel, which, own_rows(me), :],
            send_sem=send_sem.at[channel, which, step],
            recv_sem=recv_sem.at[channel, which, step],
            device_id={"ctx": peer(step)},
            device_id_type=MESH,
        )

    def outward_own(channel):
        return pltpu.make_async_copy(
            sf_ref.at[me, channel], got.at[channel, :, own_rows(me), :], own_sem.at[channel]
        )

    def inward(channel, step):
        return pltpu.make_async_remote_copy(
            src_ref=got.at[channel, 0, own_rows(peer(step)), :],
            dst_ref=back_ref.at[me, channel],
            send_sem=back_send.at[channel, step],
            recv_sem=back_recv.at[channel, step],
            device_id={"ctx": peer(step)},
            device_id_type=MESH,
        )

    def inward_own(channel):
        return pltpu.make_async_copy(
            got.at[channel, 0, own_rows(me), :], back_ref.at[me, channel], back_own.at[channel]
        )

    others = [(which, step) for which in range(2) for step in range(1, devices)]

    def lay_signal(column, carry):
        tile_s[tile_rows(column), :] = signal[:, tile(column)].astype(F32)
        return carry

    for channel in range(channels):
        for which in (1, 0):
            if fused:
                if channel == 0 and which == 0:
                    arrivals[1].wait()
                    lax.fori_loop(0, columns, lay_signal, 0, unroll=8)
                source = (tile_s, tile_f)[which]
                for device in range(devices):
                    for fold in range(folds):
                        part = pl.ds(fold * 128, 128)
                        sf_ref[device, channel, which, :, part] = source[
                            strip(device, channel, fold), :
                        ]
            for step in range(1, devices):
                outward(channel, which, step).start()
        outward_own(channel).start()
    loads = [
        pltpu.make_async_copy(source, target, table_sem.at[i])
        for i, (source, target) in enumerate(zip(tables, held))
    ]
    for load in loads:
        load.start()
    for load in loads:
        load.wait()

    def arrive(channel):
        outward_own(channel).wait()
        for which, step in others:
            outward(channel, which, step).wait_recv()

    def convolve(channel):
        high, low = split(got[channel, 1])
        wide[:, :width] = got[channel, 0].astype(BF16)
        wide[:, width : 2 * width] = high
        wide[:, 2 * width :] = low

        def one_chunk(part, carry):
            from_high = dot(fwd_hi[part], wide[...])
            from_low = dot(fwd_lo[part], wide[:, : 2 * width])
            both = from_high[:, : 2 * width] + from_low
            series = (both[:, :width], both[:, width:] + from_high[:, 2 * width :])
            cos, sin = twist[part, 0], twist[part, 1]
            turned = [
                jnp.concatenate(
                    [
                        value[:chunk] * cos - value[chunk:] * sin,
                        value[:chunk] * sin + value[chunk:] * cos,
                    ],
                    axis=1,
                )
                for value in series
            ]
            high, low = split(jnp.concatenate(turned, axis=0))
            bins = dot(high, in_hi[...]) + dot(high, in_lo[...]) + dot(low, in_hi[...])
            s_re, s_im = bins[:chunk, :width], bins[:chunk, width:]
            f_re, f_im = bins[chunk:, :width] * scale, bins[chunk:, width:] * scale
            prod = jnp.concatenate(
                [s_re * f_re - s_im * f_im, -(s_re * f_im + s_im * f_re)], axis=1
            )
            high, low = split(prod)
            back = dot(high, in_hi[...]) + dot(high, in_lo[...]) + dot(low, in_hi[...])
            b_re, b_im = back[:, :width], back[:, width:]
            high, low = split(
                jnp.concatenate([b_re * cos - b_im * sin, -(b_re * sin + b_im * cos)], axis=0)
            )
            term = dot(bwd_hi[part], high) + dot(bwd_lo[part], high) + dot(bwd_hi[part], low)

            @pl.when(part == 0)
            def _():
                got[channel, 0] = term

            @pl.when(part > 0)
            def _():
                got[channel, 0] += term

            return carry

        lax.fori_loop(0, chunks, one_chunk, 0)

    def one_channel(channel, carry):
        arrive(channel)
        convolve(channel)
        for step in range(1, devices):
            inward(channel, step).start()
        inward_own(channel).start()
        return carry

    lax.fori_loop(0, channels, one_channel, 0)
    for channel in range(channels):
        inward_own(channel).wait()
        for step in range(1, devices):
            inward(channel, step).wait_recv()
        if fused:
            for device in range(devices):
                for fold in range(folds):
                    part = pl.ds(fold * 128, 128)
                    tile_s[strip(device, channel, fold), :] = back_ref[device, channel, :, part]
    if fused:
        pieces = 4
        span = columns // pieces
        leaves = []

        def finish(column, carry):
            result[:, tile(column)] = tile_s[tile_rows(column), :]
            return carry

        for piece in range(pieces):
            lax.fori_loop(piece * span, (piece + 1) * span, finish, 0, unroll=8)
            there = pl.ds(piece * span * 128, span * 128)
            leaves.append(
                pltpu.make_async_copy(
                    result.at[:, there], out_ref.at[:, there], load_sem.at[2 + piece]
                )
            )
            leaves[-1].start()
        for leave in leaves:
            leave.wait()
    for channel in range(channels):
        for which, step in others:
            outward(channel, which, step).wait_send()
        for step in range(1, devices):
            inward(channel, step).wait_send()


def shards(signal, filter_taps, gate_values, skip_gain):
    devices = lax.axis_size("ctx")
    channels, block = signal.shape
    length = devices * block
    own = channels // devices
    second_len = 1
    while 4 * second_len * second_len <= length:
        second_len *= 2
    first_len = length // second_len
    rows = first_len // devices
    chunk = min(first_len, max(128, 131072 // first_len))
    tables = make_tables(first_len, second_len, chunk)
    inputs = signal.astype(F32)
    fused = channels * block <= 1 << 19
    shape = (devices, own, rows, second_len)
    packed_shape = (devices, own, 2, rows, second_len)
    anywhere = pl.BlockSpec(memory_space=pl.ANY)
    out_pairs = pltpu.SemaphoreType.DMA((own, 2, devices))
    pairs = pltpu.SemaphoreType.DMA((own, devices))
    singles = pltpu.SemaphoreType.DMA((own,))
    scratch = [pltpu.VMEM(table.shape, table.dtype) for table in tables] + [
        pltpu.VMEM((own, 2, first_len, second_len), F32),
        pltpu.VMEM((first_len, 3 * second_len), BF16),
        out_pairs,
        out_pairs,
        singles,
        pltpu.SemaphoreType.DMA((7,)),
        pairs,
        pairs,
        singles,
    ]
    if fused:
        scratch = [
            pltpu.VMEM((channels, block), BF16),
            pltpu.VMEM((channels, block), F32),
            pltpu.VMEM((channels, block), F32),
            pltpu.VMEM((channels * block // 128, 128), F32),
            pltpu.VMEM((channels * block // 128, 128), F32),
            pltpu.VMEM(packed_shape, F32),
            pltpu.VMEM(shape, F32),
            pltpu.SemaphoreType.DMA((6,)),
        ] + scratch
        operands = [signal, filter_taps]
        out_shape = jax.ShapeDtypeStruct((channels, block), F32)
    else:
        operands = [jnp.stack([inputs.reshape(shape), filter_taps.reshape(shape)], axis=2)]
        out_shape = jax.ShapeDtypeStruct(shape, F32)
    result = pl.pallas_call(
        functools.partial(kernel, devices, chunk, fused),
        out_shape=out_shape,
        in_specs=[pl.BlockSpec(memory_space=pltpu.HBM)] * (7 + len(operands)),
        out_specs=anywhere,
        scratch_shapes=scratch,
        compiler_params=pltpu.CompilerParams(
            collective_id=0, has_side_effects=True, vmem_limit_bytes=(40 if length <= 1 << 17 else 60) << 20
        ),
    )(*[jnp.asarray(table) for table in tables], *operands)
    long_conv = result.reshape(channels, block)
    gated = gate_values.astype(F32) * (long_conv + skip_gain[:, None] * inputs)
    return gated.astype(BF16)


def solution(mesh):
    in_specs = (P("ch", "ctx"), P("ch", "ctx"), P("ch", "ctx"), P("ch"))
    out_specs = P("ch", "ctx")
    return jax.shard_map(shards, mesh=mesh, in_specs=in_specs, out_specs=out_specs, check_vma=False)
```

```python
import functools
import math

import jax
import jax.numpy as jnp
import ml_dtypes
import numpy as np
from jax import lax
from jax.experimental import pallas as pl
from jax.experimental.pallas import tpu as pltpu
from jax.sharding import PartitionSpec as P

MESH = pl.DeviceIdType.MESH
BF16 = jnp.bfloat16
F32 = jnp.float32


def split_table(values):
    high = values.astype(ml_dtypes.bfloat16)
    low = (values - high.astype(np.float64)).astype(ml_dtypes.bfloat16)
    return high, low


def angles(rows, columns, period):
    return 2.0 * math.pi / period * (np.outer(rows, columns) % period)


def make_tables(first_len, second_len, chunk):
    chunks = first_len // chunk
    length = first_len * second_len
    first = np.arange(first_len, dtype=np.int64)
    second = np.arange(second_len, dtype=np.int64)
    quarter = 4 * first + 1
    theta = angles(quarter, first, 4 * first_len)
    forward = np.stack([np.cos(theta), -np.sin(theta)]).reshape(2, chunks, chunk, first_len)
    forward = forward.transpose(1, 0, 2, 3).reshape(chunks, 2 * chunk, first_len)
    backward = np.ascontiguousarray(forward.transpose(0, 2, 1))
    theta = angles(quarter, second, 4 * length)
    twist = np.stack([np.cos(theta), -np.sin(theta)]).reshape(2, chunks, chunk, second_len)
    twist = np.ascontiguousarray(twist.transpose(1, 0, 2, 3)).astype(np.float32)
    theta = angles(second, second, second_len)
    cos, sin = np.cos(theta), np.sin(theta)
    inner = np.block([[cos, -sin], [sin, cos]])
    return (*split_table(forward), *split_table(backward), *split_table(inner), twist)


def split(values):
    high = values.astype(BF16)
    low = (values - high.astype(F32)).astype(BF16)
    return high, low


def dot(left, right):
    return jnp.dot(left, right, preferred_element_type=F32)


def kernel(devices, chunk, fused, *refs):
    tables, rest = refs[:7], refs[7:]
    held = rest[-16:-9]
    got, wide, send_sem, recv_sem, own_sem, table_sem, back_send, back_recv, back_own = rest[-9:]
    if fused:
        signal_ref, taps_ref, out_ref = rest[:3]
        signal, taps, result, tile_s, tile_f, sf_ref, back_ref, load_sem = rest[3:-16]
    else:
        sf_ref, back_ref = rest[:2]
    fwd_hi, fwd_lo, bwd_hi, bwd_lo, in_hi, in_lo, twist = held
    me = lax.axis_index("ctx")
    _, channels, _, rows, width = sf_ref.shape
    chunks = fwd_hi.shape[0]
    scale = 1.0 / (devices * rows * width)
    folds = width // 128
    lanes = devices * channels

    def peer(step):
        return lax.rem(me + step, devices)

    if fused:
        arrivals = [
            pltpu.make_async_copy(source, target, load_sem.at[i])
            for i, (source, target) in enumerate(
                ((taps_ref, taps), (signal_ref, signal))
            )
        ]
        for arrival in arrivals:
            arrival.start()

    barrier = pltpu.get_barrier_semaphore()
    for step in range(1, devices):
        pl.semaphore_signal(barrier, inc=1, device_id={"ctx": peer(step)}, device_id_type=MESH)

    def tile(column):
        return pl.ds(pl.multiple_of(column * 128, 128), 128)

    def tile_rows(column):
        return pl.ds(pl.multiple_of(column * lanes, lanes), lanes)

    if fused:
        columns = rows * folds
        arrivals[0].wait()

        def lay_taps(column, carry):
            tile_f[tile_rows(column), :] = taps[:, tile(column)]
            return carry

        lax.fori_loop(0, columns, lay_taps, 0, unroll=8)

    pl.semaphore_wait(barrier, devices - 1)

    def strip(device, channel, fold):
        start = device * channels + channel + fold * lanes
        return pl.ds(start, rows, stride=lanes * folds)

    def own_rows(device):
        return pl.ds(pl.multiple_of(device * rows, rows), rows)

    def outward(channel, which, step):
        return pltpu.make_async_remote_copy(
            src_ref=sf_ref.at[peer(step), channel, which],
            dst_ref=got.at[channel, which, own_rows(me), :],
            send_sem=send_sem.at[channel, which, step],
            recv_sem=recv_sem.at[channel, which, step],
            device_id={"ctx": peer(step)},
            device_id_type=MESH,
        )

    def outward_own(channel):
        return pltpu.make_async_copy(
            sf_ref.at[me, channel], got.at[channel, :, own_rows(me), :], own_sem.at[channel]
        )

    def inward(channel, step):
        return pltpu.make_async_remote_copy(
            src_ref=got.at[channel, 0, own_rows(peer(step)), :],
            dst_ref=back_ref.at[me, channel],
            send_sem=back_send.at[channel, step],
            recv_sem=back_recv.at[channel, step],
            device_id={"ctx": peer(step)},
            device_id_type=MESH,
        )

    def inward_own(channel):
        return pltpu.make_async_copy(
            got.at[channel, 0, own_rows(me), :], back_ref.at[me, channel], back_own.at[channel]
        )

    others = [(which, step) for which in range(2) for step in range(1, devices)]

    def lay_signal(column, carry):
        tile_s[tile_rows(column), :] = signal[:, tile(column)].astype(F32)
        return carry

    for channel in range(channels):
        for which in (1, 0):
            if fused:
                if channel == 0 and which == 0:
                    arrivals[1].wait()
                    lax.fori_loop(0, columns, lay_signal, 0, unroll=8)
                source = (tile_s, tile_f)[which]
                for device in range(devices):
                    for fold in range(folds):
                        part = pl.ds(fold * 128, 128)
                        sf_ref[device, channel, which, :, part] = source[
                            strip(device, channel, fold), :
                        ]
            for step in range(1, devices):
                outward(channel, which, step).start()
        outward_own(channel).start()
    loads = [
        pltpu.make_async_copy(source, target, table_sem.at[i])
        for i, (source, target) in enumerate(zip(tables, held))
    ]
    for load in loads:
        load.start()
    for load in loads:
        load.wait()

    def arrive(channel):
        outward_own(channel).wait()
        for which, step in others:
            outward(channel, which, step).wait_recv()

    def convolve(channel):
        high, low = split(got[channel, 1])
        wide[:, :width] = got[channel, 0].astype(BF16)
        wide[:, width : 2 * width] = high
        wide[:, 2 * width :] = low

        def one_chunk(part, carry):
            from_high = dot(fwd_hi[part], wide[...])
            from_low = dot(fwd_lo[part], wide[:, : 2 * width])
            both = from_high[:, : 2 * width] + from_low
            series = (both[:, :width], both[:, width:] + from_high[:, 2 * width :])
            cos, sin = twist[part, 0], twist[part, 1]
            turned = [
                jnp.concatenate(
                    [
                        value[:chunk] * cos - value[chunk:] * sin,
                        value[:chunk] * sin + value[chunk:] * cos,
                    ],
                    axis=1,
                )
                for value in series
            ]
            high, low = split(jnp.concatenate(turned, axis=0))
            bins = dot(high, in_hi[...]) + dot(high, in_lo[...]) + dot(low, in_hi[...])
            s_re, s_im = bins[:chunk, :width], bins[:chunk, width:]
            f_re, f_im = bins[chunk:, :width] * scale, bins[chunk:, width:] * scale
            prod = jnp.concatenate(
                [s_re * f_re - s_im * f_im, -(s_re * f_im + s_im * f_re)], axis=1
            )
            high, low = split(prod)
            back = dot(high, in_hi[...]) + dot(high, in_lo[...]) + dot(low, in_hi[...])
            b_re, b_im = back[:, :width], back[:, width:]
            high, low = split(
                jnp.concatenate([b_re * cos - b_im * sin, -(b_re * sin + b_im * cos)], axis=0)
            )
            term = dot(bwd_hi[part], high) + dot(bwd_lo[part], high) + dot(bwd_hi[part], low)

            @pl.when(part == 0)
            def _():
                got[channel, 0] = term

            @pl.when(part > 0)
            def _():
                got[channel, 0] += term

            return carry

        lax.fori_loop(0, chunks, one_chunk, 0)

    def one_channel(channel, carry):
        arrive(channel)
        convolve(channel)
        for step in range(1, devices):
            inward(channel, step).start()
        inward_own(channel).start()
        return carry

    lax.fori_loop(0, channels, one_channel, 0)
    for channel in range(channels):
        inward_own(channel).wait()
        for step in range(1, devices):
            inward(channel, step).wait_recv()
        if fused:
            for device in range(devices):
                for fold in range(folds):
                    part = pl.ds(fold * 128, 128)
                    tile_s[strip(device, channel, fold), :] = back_ref[device, channel, :, part]
    if fused:
        pieces = 4
        span = columns // pieces
        leaves = []

        def finish(column, carry):
            result[:, tile(column)] = tile_s[tile_rows(column), :]
            return carry

        for piece in range(pieces):
            lax.fori_loop(piece * span, (piece + 1) * span, finish, 0, unroll=8)
            there = pl.ds(piece * span * 128, span * 128)
            leaves.append(
                pltpu.make_async_copy(
                    result.at[:, there], out_ref.at[:, there], load_sem.at[2 + piece]
                )
            )
            leaves[-1].start()
        for leave in leaves:
            leave.wait()
    for channel in range(channels):
        for which, step in others:
            outward(channel, which, step).wait_send()
        for step in range(1, devices):
            inward(channel, step).wait_send()


def shards(signal, filter_taps, gate_values, skip_gain):
    devices = lax.axis_size("ctx")
    channels, block = signal.shape
    length = devices * block
    own = channels // devices
    second_len = 1
    while 4 * second_len * second_len <= length:
        second_len *= 2
    first_len = length // second_len
    rows = first_len // devices
    chunk = min(first_len, max(128, 131072 // first_len))
    tables = make_tables(first_len, second_len, chunk)
    inputs = signal.astype(F32)
    fused = channels * block <= 1 << 19
    shape = (devices, own, rows, second_len)
    packed_shape = (devices, own, 2, rows, second_len)
    anywhere = pl.BlockSpec(memory_space=pl.ANY)
    out_pairs = pltpu.SemaphoreType.DMA((own, 2, devices))
    pairs = pltpu.SemaphoreType.DMA((own, devices))
    singles = pltpu.SemaphoreType.DMA((own,))
    scratch = [pltpu.VMEM(table.shape, table.dtype) for table in tables] + [
        pltpu.VMEM((own, 2, first_len, second_len), F32),
        pltpu.VMEM((first_len, 3 * second_len), BF16),
        out_pairs,
        out_pairs,
        singles,
        pltpu.SemaphoreType.DMA((7,)),
        pairs,
        pairs,
        singles,
    ]
    if fused:
        scratch = [
            pltpu.VMEM((channels, block), BF16),
            pltpu.VMEM((channels, block), F32),
            pltpu.VMEM((channels, block), F32),
            pltpu.VMEM((channels * block // 128, 128), F32),
            pltpu.VMEM((channels * block // 128, 128), F32),
            pltpu.VMEM(packed_shape, F32),
            pltpu.VMEM(shape, F32),
            pltpu.SemaphoreType.DMA((6,)),
        ] + scratch
        operands = [signal, filter_taps]
        out_shape = jax.ShapeDtypeStruct((channels, block), F32)
    else:
        operands = [jnp.stack([inputs.reshape(shape), filter_taps.reshape(shape)], axis=2)]
        out_shape = jax.ShapeDtypeStruct(shape, F32)
    operands = [jnp.asarray(table) for table in tables] + operands
    result = pl.pallas_call(
        functools.partial(kernel, devices, chunk, fused),
        out_shape=out_shape,
        in_specs=[pl.BlockSpec(memory_space=pltpu.HBM)] * len(operands),
        out_specs=anywhere,
        scratch_shapes=scratch,
        compiler_params=pltpu.CompilerParams(
            collective_id=0, has_side_effects=True, vmem_limit_bytes=(40 if length <= 1 << 17 else 60) << 20
        ),
    )(*[pltpu.with_memory_space_constraint(operand, pltpu.HBM) for operand in operands])
    long_conv = result.reshape(channels, block)
    gated = gate_values.astype(F32) * (long_conv + skip_gain[:, None] * inputs)
    return gated.astype(BF16)


def solution(mesh):
    in_specs = (P("ch", "ctx"), P("ch", "ctx"), P("ch", "ctx"), P("ch"))
    out_specs = P("ch", "ctx")
    return jax.shard_map(shards, mesh=mesh, in_specs=in_specs, out_specs=out_specs, check_vma=False)
```

```python
import functools
import math

import jax
import jax.numpy as jnp
import ml_dtypes
import numpy as np
from jax import lax
from jax.experimental import pallas as pl
from jax.experimental.pallas import tpu as pltpu
from jax.sharding import PartitionSpec as P

MESH = pl.DeviceIdType.MESH
BF16 = jnp.bfloat16
F32 = jnp.float32


def split_table(values):
    high = values.astype(ml_dtypes.bfloat16)
    low = (values - high.astype(np.float64)).astype(ml_dtypes.bfloat16)
    return high, low


def angles(rows, columns, period):
    return 2.0 * math.pi / period * (np.outer(rows, columns) % period)


def make_tables(first_len, second_len, chunk):
    chunks = first_len // chunk
    length = first_len * second_len
    first = np.arange(first_len, dtype=np.int64)
    second = np.arange(second_len, dtype=np.int64)
    quarter = 4 * first + 1
    theta = angles(quarter, first, 4 * first_len)
    forward = np.stack([np.cos(theta), -np.sin(theta)]).reshape(2, chunks, chunk, first_len)
    forward = forward.transpose(1, 0, 2, 3).reshape(chunks, 2 * chunk, first_len)
    backward = np.ascontiguousarray(forward.transpose(0, 2, 1))
    theta = angles(quarter, second, 4 * length)
    twist = np.stack([np.cos(theta), -np.sin(theta)]).reshape(2, chunks, chunk, second_len)
    twist = np.ascontiguousarray(twist.transpose(1, 0, 2, 3)).astype(np.float32)
    theta = angles(second, second, second_len)
    cos, sin = np.cos(theta), np.sin(theta)
    inner = np.block([[cos, -sin], [sin, cos]])
    return (*split_table(forward), *split_table(backward), *split_table(inner), twist)


def split(values):
    high = values.astype(BF16)
    low = (values - high.astype(F32)).astype(BF16)
    return high, low


def dot(left, right):
    return jnp.dot(left, right, preferred_element_type=F32)


def kernel(devices, chunk, fused, *refs):
    tables, rest = refs[:7], refs[7:]
    held = rest[-16:-9]
    got, wide, send_sem, recv_sem, own_sem, table_sem, back_send, back_recv, back_own = rest[-9:]
    if fused:
        signal_ref, taps_ref, out_ref = rest[:3]
        signal, taps, tile_s, tile_f, sf_ref, back_ref, load_sem = rest[3:-16]
    else:
        sf_ref, back_ref = rest[:2]
    fwd_hi, fwd_lo, bwd_hi, bwd_lo, in_hi, in_lo, twist = held
    me = lax.axis_index("ctx")
    _, channels, _, rows, width = sf_ref.shape
    chunks = fwd_hi.shape[0]
    scale = 1.0 / (devices * rows * width)
    folds = width // 128
    lanes = devices * channels

    def peer(step):
        return lax.rem(me + step, devices)

    if fused:
        arrivals = [
            pltpu.make_async_copy(source, target, load_sem.at[i])
            for i, (source, target) in enumerate(
                ((taps_ref, taps), (signal_ref, signal))
            )
        ]
        for arrival in arrivals:
            arrival.start()

    barrier = pltpu.get_barrier_semaphore()
    for step in range(1, devices):
        pl.semaphore_signal(barrier, inc=1, device_id={"ctx": peer(step)}, device_id_type=MESH)

    def tile(column):
        return pl.ds(pl.multiple_of(column * 128, 128), 128)

    def tile_rows(column):
        return pl.ds(pl.multiple_of(column * lanes, lanes), lanes)

    if fused:
        columns = rows * folds
        arrivals[0].wait()

        def lay_taps(column, carry):
            tile_f[tile_rows(column), :] = taps[:, tile(column)]
            return carry

        lax.fori_loop(0, columns, lay_taps, 0, unroll=8)

    pl.semaphore_wait(barrier, devices - 1)

    def strip(device, channel, fold):
        start = device * channels + channel + fold * lanes
        return pl.ds(start, rows, stride=lanes * folds)

    def own_rows(device):
        return pl.ds(pl.multiple_of(device * rows, rows), rows)

    def outward(channel, which, step):
        return pltpu.make_async_remote_copy(
            src_ref=sf_ref.at[peer(step), channel, which],
            dst_ref=got.at[channel, which, own_rows(me), :],
            send_sem=send_sem.at[channel, which, step],
            recv_sem=recv_sem.at[channel, which, step],
            device_id={"ctx": peer(step)},
            device_id_type=MESH,
        )

    def outward_own(channel):
        return pltpu.make_async_copy(
            sf_ref.at[me, channel], got.at[channel, :, own_rows(me), :], own_sem.at[channel]
        )

    def inward(channel, step):
        return pltpu.make_async_remote_copy(
            src_ref=got.at[channel, 0, own_rows(peer(step)), :],
            dst_ref=back_ref.at[me, channel],
            send_sem=back_send.at[channel, step],
            recv_sem=back_recv.at[channel, step],
            device_id={"ctx": peer(step)},
            device_id_type=MESH,
        )

    def inward_own(channel):
        return pltpu.make_async_copy(
            got.at[channel, 0, own_rows(me), :], back_ref.at[me, channel], back_own.at[channel]
        )

    others = [(which, step) for which in range(2) for step in range(1, devices)]

    def lay_signal(column, carry):
        tile_s[tile_rows(column), :] = signal[:, tile(column)].astype(F32)
        return carry

    for channel in range(channels):
        for which in (1, 0):
            if fused:
                if channel == 0 and which == 0:
                    arrivals[1].wait()
                    lax.fori_loop(0, columns, lay_signal, 0, unroll=8)
                source = (tile_s, tile_f)[which]
                for device in range(devices):
                    for fold in range(folds):
                        part = pl.ds(fold * 128, 128)
                        sf_ref[device, channel, which, :, part] = source[
                            strip(device, channel, fold), :
                        ]
            for step in range(1, devices):
                outward(channel, which, step).start()
        outward_own(channel).start()
    loads = [
        pltpu.make_async_copy(source, target, table_sem.at[i])
        for i, (source, target) in enumerate(zip(tables, held))
    ]
    for load in loads:
        load.start()
    for load in loads:
        load.wait()

    def arrive(channel):
        outward_own(channel).wait()
        for which, step in others:
            outward(channel, which, step).wait_recv()

    def convolve(channel):
        high, low = split(got[channel, 1])
        wide[:, :width] = got[channel, 0].astype(BF16)
        wide[:, width : 2 * width] = high
        wide[:, 2 * width :] = low

        def one_chunk(part, carry):
            from_high = dot(fwd_hi[part], wide[...])
            from_low = dot(fwd_lo[part], wide[:, : 2 * width])
            both = from_high[:, : 2 * width] + from_low
            series = (both[:, :width], both[:, width:] + from_high[:, 2 * width :])
            cos, sin = twist[part, 0], twist[part, 1]
            turned = [
                jnp.concatenate(
                    [
                        value[:chunk] * cos - value[chunk:] * sin,
                        value[:chunk] * sin + value[chunk:] * cos,
                    ],
                    axis=1,
                )
                for value in series
            ]
            high, low = split(jnp.concatenate(turned, axis=0))
            bins = dot(high, in_hi[...]) + dot(high, in_lo[...]) + dot(low, in_hi[...])
            s_re, s_im = bins[:chunk, :width], bins[:chunk, width:]
            f_re, f_im = bins[chunk:, :width] * scale, bins[chunk:, width:] * scale
            prod = jnp.concatenate(
                [s_re * f_re - s_im * f_im, -(s_re * f_im + s_im * f_re)], axis=1
            )
            high, low = split(prod)
            back = dot(high, in_hi[...]) + dot(high, in_lo[...]) + dot(low, in_hi[...])
            b_re, b_im = back[:, :width], back[:, width:]
            high, low = split(
                jnp.concatenate([b_re * cos - b_im * sin, -(b_re * sin + b_im * cos)], axis=0)
            )
            term = dot(bwd_hi[part], high) + dot(bwd_lo[part], high) + dot(bwd_hi[part], low)

            @pl.when(part == 0)
            def _():
                got[channel, 0] = term

            @pl.when(part > 0)
            def _():
                got[channel, 0] += term

            return carry

        lax.fori_loop(0, chunks, one_chunk, 0)

    def one_channel(channel, carry):
        arrive(channel)
        convolve(channel)
        for step in range(1, devices):
            inward(channel, step).start()
        inward_own(channel).start()
        return carry

    lax.fori_loop(0, channels, one_channel, 0)
    for channel in range(channels):
        inward_own(channel).wait()
        for step in range(1, devices):
            inward(channel, step).wait_recv()
        if fused:
            for device in range(devices):
                for fold in range(folds):
                    part = pl.ds(fold * 128, 128)
                    tile_s[strip(device, channel, fold), :] = back_ref[device, channel, :, part]
    if fused:

        def finish(column, carry):
            out_ref[:, tile(column)] = tile_s[tile_rows(column), :]
            return carry

        lax.fori_loop(0, columns, finish, 0, unroll=8)
    for channel in range(channels):
        for which, step in others:
            outward(channel, which, step).wait_send()
        for step in range(1, devices):
            inward(channel, step).wait_send()


def shards(signal, filter_taps, gate_values, skip_gain):
    devices = lax.axis_size("ctx")
    channels, block = signal.shape
    length = devices * block
    own = channels // devices
    second_len = 1
    while 4 * second_len * second_len <= length:
        second_len *= 2
    first_len = length // second_len
    rows = first_len // devices
    chunk = min(first_len, max(128, 131072 // first_len))
    tables = make_tables(first_len, second_len, chunk)
    inputs = signal.astype(F32)
    fused = channels * block <= 1 << 19
    shape = (devices, own, rows, second_len)
    packed_shape = (devices, own, 2, rows, second_len)
    anywhere = pl.BlockSpec(memory_space=pl.ANY)
    out_pairs = pltpu.SemaphoreType.DMA((own, 2, devices))
    pairs = pltpu.SemaphoreType.DMA((own, devices))
    singles = pltpu.SemaphoreType.DMA((own,))
    scratch = [pltpu.VMEM(table.shape, table.dtype) for table in tables] + [
        pltpu.VMEM((own, 2, first_len, second_len), F32),
        pltpu.VMEM((first_len, 3 * second_len), BF16),
        out_pairs,
        out_pairs,
        singles,
        pltpu.SemaphoreType.DMA((7,)),
        pairs,
        pairs,
        singles,
    ]
    if fused:
        scratch = [
            pltpu.VMEM((channels, block), BF16),
            pltpu.VMEM((channels, block), F32),
            pltpu.VMEM((channels * block // 128, 128), F32),
            pltpu.VMEM((channels * block // 128, 128), F32),
            pltpu.VMEM(packed_shape, F32),
            pltpu.VMEM(shape, F32),
            pltpu.SemaphoreType.DMA((2,)),
        ] + scratch
        operands = [signal, filter_taps]
        out_shape = jax.ShapeDtypeStruct((channels, block), F32)
    else:
        operands = [jnp.stack([inputs.reshape(shape), filter_taps.reshape(shape)], axis=2)]
        out_shape = jax.ShapeDtypeStruct(shape, F32)
    operands = [jnp.asarray(table) for table in tables] + operands
    result = pl.pallas_call(
        functools.partial(kernel, devices, chunk, fused),
        out_shape=out_shape,
        in_specs=[pl.BlockSpec(memory_space=pltpu.HBM)] * len(operands),
        out_specs=pl.BlockSpec(memory_space=pltpu.VMEM if fused else pl.ANY),
        scratch_shapes=scratch,
        compiler_params=pltpu.CompilerParams(
            collective_id=0, has_side_effects=True, vmem_limit_bytes=(40 if length <= 1 << 17 else 60) << 20
        ),
    )(*[pltpu.with_memory_space_constraint(operand, pltpu.HBM) for operand in operands])
    long_conv = result.reshape(channels, block)
    gated = gate_values.astype(F32) * (long_conv + skip_gain[:, None] * inputs)
    return gated.astype(BF16)


def solution(mesh):
    in_specs = (P("ch", "ctx"), P("ch", "ctx"), P("ch", "ctx"), P("ch"))
    out_specs = P("ch", "ctx")
    return jax.shard_map(shards, mesh=mesh, in_specs=in_specs, out_specs=out_specs, check_vma=False)
```
